512 devices in a mesh: sec: 4 (over x), tile: 128 (over y, z, core).
Axes of the slice: x: 4, y: 8, z: 8, core: 2. Of those that a mesh axis runs over, the one named last changes fastest.
Arguments:
- pre_act: bfloat16 [4, 131072, 512], P('sec', 'tile'), may hold values from -6 to 6
- edge_cot: bfloat16 [4, 131072, 512], P('sec', 'tile'), may hold values from -4 to 4
- recv_local: int32 [4, 131072], P('sec', 'tile'), may hold values from 0 to 127
- send_slot: int32 [4, 131072], P('sec', 'tile'), may hold values from 0 to 639
- edge_count: int32 [4, 128], P('sec', 'tile'), may hold values from 256 to 1024, as said below
- halo_map: int32 [4, 128, 128], P('sec', 'tile'), may hold values from 0 to 511
- dec_rows: bfloat16 [4, 65536, 512], P('sec', 'tile'), may hold values from -4 to 4
- dec_count: int32 [4, 1024], P('sec', 'tile'), may hold values from 1 to 64, as said below
- dec_node: int32 [4, 65536], P('sec', 'tile'), may hold values from 0 to 127, as said below
- w_node: bfloat16 [1024, 512], replicated, may hold values from -0.15625 to 0.15625
- w_out: bfloat16 [512, 512], replicated, may hold values from -0.25 to 0.25
Outputs:
- node_grad: float32 [4, 16384, 512], P('sec', 'tile')
The draws below stay inside these ranges and needn't reach their ends.
Inputs may be any that keep to these rules, and one draw needn't show every extreme that they name: `edge_count`: some device has all 1024 edge slots live. `dec_count`: in each block q one offset has 64 live rows from every source tile. `dec_node`: rows c and c2 of one destination and offset with c // 4 == c2 // 4 name the same node.
All inputs are finite; a program needn't handle non-finite values.
Results may differ from the reference program's by a relative error of at most 0.0035.
Values may be sent and summed in bfloat16 or wider, within the bound.
A program may use at most 64 MiB of HBM per device.

```python
import jax
import jax.numpy as jnp
from jax import lax

D = 512
QUART = 128
EDGE_DEV = 1024
CAP = 64
GROUP = 4
NEIGH = 8
HCAP = 16
EDGES_ROW = 131072
DEC_ROWS = 65536
HALO = 128
N_SEC = 4
N_TILE = 128


def draw_send_slot(key, part):
    key = jax.random.fold_in(key, 11)
    key_local, key_offset, key_slot, key_pick = jax.random.split(key, 4)
    grid_shape = (N_SEC, N_TILE * EDGE_DEV)
    local_col = jax.random.randint(key_local, grid_shape, 0, N_SEC * QUART)
    offset_number = jax.random.randint(key_offset, grid_shape, 0, NEIGH)
    halo_slot = jax.random.randint(key_slot, grid_shape, 0, HCAP)
    remote_col = N_SEC * QUART + offset_number * HCAP + halo_slot
    pick_far = jax.random.randint(key_pick, grid_shape, 0, 4) == 0
    return jnp.where(pick_far, remote_col, local_col).astype(jnp.int32)


def draw_edge_count(key, part):
    key = jax.random.fold_in(key, 12)
    key_value, key_full = jax.random.split(key)
    grid_shape = (N_SEC, N_TILE)
    values = jax.random.randint(key_value, grid_shape, EDGE_DEV // 4, EDGE_DEV + 1)
    full_one = jax.random.randint(key_full, (), 0, N_SEC * N_TILE)
    flat_index = lax.broadcasted_iota(jnp.int32, grid_shape, 0) * N_TILE + lax.broadcasted_iota(jnp.int32, grid_shape, 1)
    return jnp.where(flat_index == full_one, EDGE_DEV, values).astype(jnp.int32)


def draw_dec_count(key, part):
    key = jax.random.fold_in(key, 13)
    key_value, key_busy = jax.random.split(key)
    grid_shape = (N_SEC, N_TILE * NEIGH)
    values = jax.random.randint(key_value, grid_shape, 1, CAP + 1)
    busy_offset = jax.random.randint(key_busy, (N_SEC, 1), 0, NEIGH)
    offset_number = lax.broadcasted_iota(jnp.int32, grid_shape, 1) % NEIGH
    return jnp.where(offset_number == busy_offset, CAP, values).astype(jnp.int32)


def draw_dec_node(key, part):
    key = jax.random.fold_in(key, 14)
    grouped = jax.random.randint(key, (N_SEC, N_TILE * NEIGH * CAP // GROUP), 0, QUART)
    return jnp.repeat(grouped, GROUP, axis=1).astype(jnp.int32)


def with_ends(array, key, smallest, top_value):
    spot = [jax.random.randint(jax.random.fold_in(key, axis), (), 0, length) for axis, length in enumerate(array.shape)]
    widest = array.shape.index(max(array.shape))
    next_to = spot[:widest] + [(spot[widest] + 1) % array.shape[widest]] + spot[widest + 1:]
    return array.at[tuple(spot)].set(smallest).at[tuple(next_to)].set(top_value)


def block_scale(own_key, extent, cuts, low, top_value):
    factor_of, own = 1.0, jax.random.fold_in(own_key, 6)
    for dim, parts in cuts:
        steps = jnp.exp(jax.random.uniform(jax.random.fold_in(own, dim), (parts,), jnp.float32, low / len(cuts), top_value / len(cuts)))
        factor_of = factor_of * jnp.repeat(steps, extent[dim] // parts).reshape([-1 if axis == dim else 1 for axis in range(len(extent))])
    return factor_of


def scatter_about(rng, dims, width, reach, shards=(), kind=jnp.bfloat16):
    values = jax.random.normal(rng, dims, jnp.float32) * width
    if len(shards) > 0:
        values = block_scale(rng, dims, shards, -0.22, 0.18) * values
    return jnp.clip(values, min=-reach, max=reach).astype(kind)


def setup_inputs(seed: int = 0) -> dict:
    streams_of = jax.random.split(jax.random.key(seed), 12)
    return {
        "pre_act": scatter_about(streams_of[0], (N_SEC, EDGES_ROW, D), 1.5, 6.0, ((0, 4), (1, 128))),
        "edge_cot": scatter_about(streams_of[1], (N_SEC, EDGES_ROW, D), 0.5, 4.0, ((0, 4), (1, 128))),
        "recv_local": with_ends(jax.random.randint(streams_of[2], (N_SEC, EDGES_ROW), 0, QUART), jax.random.fold_in(streams_of[2], 1), 0, QUART - 1).astype(jnp.int32),
        "send_slot": draw_send_slot(jax.random.fold_in(streams_of[11], 71), 0),
        "edge_count": draw_edge_count(jax.random.fold_in(streams_of[11], 71), 0),
        "halo_map": with_ends(jax.random.randint(streams_of[5], (N_SEC, N_TILE, HALO), 0, N_SEC * QUART), jax.random.fold_in(streams_of[5], 1), 0, (N_SEC * QUART) - 1).astype(jnp.int32),
        "dec_rows": scatter_about(streams_of[6], (N_SEC, DEC_ROWS, D), 0.5, 4.0, ((0, 4), (1, 128))),
        "dec_count": draw_dec_count(jax.random.fold_in(streams_of[11], 71), 0),
        "dec_node": draw_dec_node(jax.random.fold_in(streams_of[11], 71), 0),
        "w_node": scatter_about(streams_of[9], (2 * D, D), (3 * D) ** -0.5, 0.15625),
        "w_out": scatter_about(streams_of[10], (D, D), D ** -0.5, 0.25),
    }


def offset_of(number):
    return (number - NEIGH // 2 + (number >= NEIGH // 2).astype(jnp.int32)).astype(jnp.int32)


def reference(pre_act, edge_cot, recv_local, send_slot, edge_count, halo_map, dec_rows, dec_count, dec_node, w_node, w_out):
    tile_nodes = N_TILE * QUART
    dec_block = dec_rows.reshape(N_SEC, N_TILE, NEIGH, CAP, D)
    grid_dims = (N_SEC, N_TILE, NEIGH, CAP)
    live_dec = lax.broadcasted_iota(jnp.int32, grid_dims, 3) < dec_count.reshape(N_SEC, N_TILE, NEIGH, 1)
    source_grid = lax.broadcasted_iota(jnp.int32, (N_TILE, NEIGH), 0)
    offset_grid = lax.broadcasted_iota(jnp.int32, (N_TILE, NEIGH), 1)
    dest_grid = ((source_grid + offset_of(offset_grid)) % N_TILE).astype(jnp.int32)
    node_table = dec_node.reshape(N_SEC, N_TILE, NEIGH, CAP)
    node_pick = node_table[:, dest_grid, offset_grid, :]
    target_node = (dest_grid[None, :, :, None] * QUART + node_pick).astype(jnp.int32)

    def decode_one(inputs):
        block_one, live_one, index_one = inputs
        values = jnp.where(live_one[..., None], block_one.astype(jnp.float32), jnp.float32(0.0))
        return jax.ops.segment_sum(values.reshape(-1, D), index_one.reshape(-1), num_segments=tile_nodes)

    node_cot = lax.map(decode_one, (dec_block, live_dec, target_node))

    position = lax.broadcasted_iota(jnp.int32, (N_TILE * EDGE_DEV,), 0)
    edge_tile = position // EDGE_DEV
    local_rows = N_SEC * QUART

    def sweep(carry, inputs):
        sec_index, preact_raw, cot_one, receiver, slot_one, count_one, halo_table, node_one = inputs
        node_low = node_one.astype(jnp.bfloat16)
        recv_global = (edge_tile * QUART + receiver).astype(jnp.int32)
        delta_act = jnp.dot(node_low[recv_global], w_out.T, preferred_element_type=jnp.float32)
        delta_act = delta_act + jnp.dot(cot_one, w_out.T, preferred_element_type=jnp.float32)
        preact = preact_raw.astype(jnp.float32)
        logistic = jax.nn.sigmoid(preact)
        slope_act = logistic * (1.0 + preact * (1.0 - logistic))
        live_edge = (position % EDGE_DEV) < count_one[edge_tile]
        delta_pre = jnp.where(live_edge[:, None], delta_act * slope_act, jnp.float32(0.0)).astype(jnp.bfloat16)
        delta_in = jnp.dot(delta_pre, w_node.T, preferred_element_type=jnp.float32)
        grad_send = lax.optimization_barrier(delta_in[:, :D].astype(jnp.bfloat16)).astype(jnp.float32)
        grad_recv = lax.optimization_barrier(delta_in[:, D:].astype(jnp.bfloat16)).astype(jnp.float32)
        recv_index = (sec_index * tile_nodes + recv_global).astype(jnp.int32)
        is_local = slot_one < local_rows
        local_global = (slot_one // QUART) * tile_nodes + edge_tile * QUART + slot_one % QUART
        halo_col = jnp.clip(slot_one - local_rows, 0, NEIGH * HCAP - 1)
        offset_number = (halo_col // HCAP).astype(jnp.int32)
        halo_slot = halo_col % HCAP
        peer_tile = ((edge_tile + offset_of(offset_number)) % N_TILE).astype(jnp.int32)
        mapped = halo_table[peer_tile, offset_number * HCAP + halo_slot]
        remote_global = (mapped // QUART) * tile_nodes + peer_tile * QUART + mapped % QUART
        send_global = jnp.where(is_local, local_global, remote_global).astype(jnp.int32)
        carry = carry.at[recv_index].add(grad_recv)
        carry = carry.at[send_global].add(grad_send)
        return carry, None

    start = jnp.zeros((N_SEC * tile_nodes, D), jnp.float32)
    sec_ids = jnp.arange(N_SEC, dtype=jnp.int32)
    total, _ = lax.scan(sweep, start, (sec_ids, pre_act, edge_cot, recv_local, send_slot, edge_count, halo_map, node_cot))
    return total.reshape(N_SEC, tile_nodes, D) + node_cot
```

```python
import functools

import jax
import jax.numpy as jnp
from jax import lax
from jax.experimental import pallas as pl
from jax.experimental.pallas import tpu as pltpu
from jax.sharding import PartitionSpec as P

MESH = pl.DeviceIdType.MESH
QUART = 128
GROUP = 4
NT = (((1,), (1,)), ((), ()))
F32 = jnp.float32
BF16 = jnp.bfloat16


def offset_value(number, neighbours):
    half = neighbours // 2
    return number - half + 1 if number >= half else number - half


def iota(shape, dim):
    return lax.broadcasted_iota(jnp.int32, shape, dim)


def hot(mask):
    return jnp.where(mask, F32(1.0), F32(0.0)).astype(BF16)


def dot(a, b):
    return jnp.dot(a, b, preferred_element_type=F32)


def dot_nt(a, b):
    return lax.dot_general(a, b, NT, preferred_element_type=F32)


def kernel(
    sec_count,
    tile_count,
    neighbours,
    pre_hbm,
    cot_hbm,
    recv_hbm,
    slot_hbm,
    ecnt_hbm,
    hmap_hbm,
    dec_hbm,
    dcnt_hbm,
    dnode_hbm,
    wnode_hbm,
    wout_hbm,
    out_ref,
    pre,
    cot,
    recv,
    slot,
    ecnt,
    hmap,
    dec,
    dcnt,
    dnode,
    wnode,
    wout,
    edge_proj,
    slope,
    delta,
    hot_edge,
    hot_sums,
    hot_dec,
    hot_land,
    node_split,
    node_cot,
    base,
    sums,
    dec_out,
    dec_in,
    halo_out,
    halo_in,
    ring_out,
    ring_in,
    load_sem,
    dec_send,
    dec_recv,
    halo_send,
    halo_recv,
    ring_send,
    ring_recv,
):
    edges, latent = cot.shape
    rows = dec.shape[0]
    groups = dec_in.shape[0]
    block = groups // neighbours
    capacity = rows // neighbours
    halo = halo_in.shape[0]
    half = latent // 2
    local_rows = sec_count * QUART
    sec = lax.axis_index("sec")
    tile = lax.axis_index("tile")
    right = lax.rem(sec + 1, sec_count)
    left = lax.rem(sec + sec_count - 1, sec_count)
    peers = [
        lax.rem(tile + offset_value(o, neighbours) + tile_count, tile_count)
        for o in range(neighbours)
    ]

    sources = [
        (dec_hbm.at[0], dec),
        (dcnt_hbm, dcnt),
        (cot_hbm.at[0], cot),
        (wout_hbm, wout),
        (pre_hbm.at[0], pre),
        (recv_hbm, recv),
        (slot_hbm, slot),
        (ecnt_hbm, ecnt),
        (dnode_hbm, dnode),
        (hmap_hbm.at[0], hmap),
        (wnode_hbm, wnode),
    ]
    loads = [
        pltpu.make_async_copy(src, dst, load_sem.at[i]) for i, (src, dst) in enumerate(sources)
    ]
    for load in loads:
        load.start()

    barrier = pltpu.get_barrier_semaphore()
    for peer in peers:
        pl.semaphore_signal(barrier, inc=1, device_id=(sec, peer), device_id_type=MESH)
    for peer in (left, right):
        pl.semaphore_signal(barrier, inc=1, device_id=(peer, tile), device_id_type=MESH)

    loads[1].wait()
    loads[0].wait()
    lane = iota((1, rows), 1)
    count = jnp.zeros((1, rows), jnp.int32)
    for o in range(neighbours):
        count = jnp.where(lane // capacity == o, dcnt[0:1, o : o + 1], count)
    live_lane = jnp.where(lane % capacity < count, lane // GROUP, -1)
    pick = hot(iota((groups, rows), 0) == live_lane)
    dec_out[...] = dot(pick, dec[...]).astype(BF16)

    pl.semaphore_wait(barrier, neighbours + 2)

    def tile_copies(src, dst, send, recv_sems):
        return [
            pltpu.make_async_remote_copy(
                src_ref=src.at[pl.ds(o * block, block)],
                dst_ref=dst.at[pl.ds(o * block, block)],
                send_sem=send.at[o],
                recv_sem=recv_sems.at[o],
                device_id=(sec, peers[o]),
                device_id_type=MESH,
            )
            for o in range(neighbours)
        ]

    dec_copies = tile_copies(dec_out, dec_in, dec_send, dec_recv)
    for copy in dec_copies:
        copy.start()

    for load in loads[2:10]:
        load.wait()
    step = 256

    def edge_block(i, carry):
        at = pl.ds(i * step, step)
        edge_proj[at, :] = dot_nt(cot[at, :], wout[...])
        v = pre[at, :].astype(F32)
        s = jax.nn.sigmoid(v)
        slope[at, :] = s * (1.0 + v * (1.0 - s))
        return carry

    lax.fori_loop(0, edges // step, edge_block, 0)

    node_row = iota((QUART, edges), 0)
    receivers = recv[...]
    edge_hot = jnp.where(node_row == receivers, F32(1.0), F32(0.0)).T.astype(BF16)
    hot_edge[:, :QUART] = edge_hot
    hot_edge[:, QUART:] = edge_hot
    live = iota((1, edges), 1) < ecnt[...]
    live_slot = jnp.where(live, slot[...], -1)
    live_recv = jnp.where(live, receivers, -1)
    hot_sums[0:QUART, :] = hot(node_row == live_slot - local_rows)
    order = (2, 1, 3, 0)
    for i, k in enumerate(order):
        quarter = lax.rem(sec + k, sec_count)
        hot_sums[(i + 1) * QUART : (i + 2) * QUART, :] = hot(
            node_row == live_slot - quarter * QUART
        )
        hot_land[i * QUART : (i + 1) * QUART, :] = hot(
            iota((QUART, halo), 0) == hmap[...] - quarter * QUART
        )
    hot_sums[5 * QUART : 6 * QUART, :] = hot(node_row == live_recv)
    first_of_group = jnp.where(lane % GROUP == 0, dnode[...], -1)
    named = hot(iota((QUART, rows), 0) == first_of_group)
    group_of = hot(iota((groups, rows), 0) == lane // GROUP)
    hot_dec[...] = dot_nt(named, group_of).astype(BF16)

    for copy in dec_copies:
        copy.wait_recv()
    cot_sum = dot(hot_dec[...], dec_in[...])
    node_cot[...] = cot_sum
    node_proj = dot_nt(cot_sum.astype(BF16), wout[...])
    high = node_proj.astype(BF16)
    node_split[:QUART, :] = high
    node_split[QUART:, :] = (node_proj - high.astype(F32)).astype(BF16)

    def delta_block(i, carry):
        at = pl.ds(i * step, step)
        act = edge_proj[at, :] + dot(hot_edge[at, :], node_split[...])
        delta[at, :] = (act * slope[at, :]).astype(BF16)
        return carry

    lax.fori_loop(0, edges // step, delta_block, 0)

    halo_out[...] = dot(hot_sums[0:QUART, :], delta[...]).astype(BF16)
    halo_copies = tile_copies(halo_out, halo_in, halo_send, halo_recv)
    for copy in halo_copies:
        copy.start()

    def sum_block(i, carry):
        at = pl.ds(i * QUART, QUART)
        sums[at, :] = dot(hot_sums[pl.ds((i + 1) * QUART, QUART), :], delta[...])
        return carry

    lax.fori_loop(0, 5, sum_block, 0)

    loads[10].wait()
    for copy in halo_copies:
        copy.wait_recv()

    def ring_copy(i, peer):
        return pltpu.make_async_remote_copy(
            src_ref=ring_out.at[i],
            dst_ref=ring_in.at[i],
            send_sem=ring_send.at[i],
            recv_sem=ring_recv.at[i],
            device_id=(peer, tile),
            device_id_type=MESH,
        )

    ring = [ring_copy(i, right if i % 2 == 0 else left) for i in range(6)]

    def with_landed(i):
        at = slice(i * QUART, (i + 1) * QUART)
        return sums[at, :] + dot(hot_land[at, :], halo_in[...])

    far = with_landed(0)
    ring_out[0] = far[:, :half].astype(BF16)
    ring_out[1] = far[:, half:].astype(BF16)
    ring[0].start()
    ring[1].start()
    ahead = with_landed(1)
    ring_out[2] = ahead[:, half:].astype(BF16)
    ring[2].start()
    behind = with_landed(2)
    ring_out[3] = behind[:, :half].astype(BF16)
    ring[3].start()
    ring[0].wait_recv()
    ring_out[4] = (ahead[:, :half] + ring_in[0].astype(F32)).astype(BF16)
    ring[4].start()
    ring[1].wait_recv()
    ring_out[5] = (behind[:, half:] + ring_in[1].astype(F32)).astype(BF16)
    ring[5].start()

    sums[3 * QUART : 4 * QUART, :] = with_landed(3)
    received = sums[4 * QUART : 5 * QUART, :].astype(BF16)
    base[...] = node_cot[...] + dot_nt(received, wnode[latent:, :])
    for i in (2, 3, 4, 5):
        ring[i].wait_recv()
    own = sums[3 * QUART : 4 * QUART, :]
    own_a = own[:, :half] + ring_in[3].astype(F32) + ring_in[4].astype(F32)
    own_b = own[:, half:] + ring_in[2].astype(F32) + ring_in[5].astype(F32)
    out_ref[0] = (
        base[...]
        + dot_nt(own_a.astype(BF16), wnode[:latent, :half])
        + dot_nt(own_b.astype(BF16), wnode[:latent, half:])
    )
    for copy in dec_copies + halo_copies + ring:
        copy.wait_send()


def per_device(
    pre_act,
    edge_cot,
    recv_local,
    send_slot,
    edge_count,
    halo_map,
    dec_rows,
    dec_count,
    dec_node,
    w_node,
    w_out,
):
    sec_count = lax.axis_size("sec")
    tile_count = lax.axis_size("tile")
    edges, latent = pre_act.shape[1:]
    rows = dec_rows.shape[1]
    neighbours = dec_count.shape[1]
    groups = rows // GROUP
    halo = halo_map.shape[2]
    half = latent // 2
    operands = (
        pre_act,
        edge_cot,
        recv_local,
        send_slot,
        edge_count,
        halo_map,
        dec_rows,
        dec_count,
        dec_node,
        w_node,
        w_out,
    )
    vmem = pltpu.VMEM
    return pl.pallas_call(
        functools.partial(kernel, sec_count, tile_count, neighbours),
        out_shape=jax.ShapeDtypeStruct((1, QUART, latent), F32),
        in_specs=[pl.BlockSpec(memory_space=pl.ANY)] * len(operands),
        out_specs=pl.BlockSpec(memory_space=pltpu.VMEM),
        scratch_shapes=[
            vmem((edges, latent), BF16),
            vmem((edges, latent), BF16),
            vmem((1, edges), jnp.int32),
            vmem((1, edges), jnp.int32),
            vmem((1, 1), jnp.int32),
            vmem((1, halo), jnp.int32),
            vmem((rows, latent), BF16),
            vmem((1, neighbours), jnp.int32),
            vmem((1, rows), jnp.int32),
            vmem(w_node.shape, BF16),
            vmem(w_out.shape, BF16),
            vmem((edges, latent), F32),
            vmem((edges, latent), F32),
            vmem((edges, latent), BF16),
            vmem((edges, 2 * QUART), BF16),
            vmem((6 * QUART, edges), BF16),
            vmem((QUART, groups), BF16),
            vmem((sec_count * QUART, halo), BF16),
            vmem((2 * QUART, latent), BF16),
            vmem((QUART, latent), F32),
            vmem((QUART, latent), F32),
            vmem((5 * QUART, latent), F32),
            vmem((groups, latent), BF16),
            vmem((groups, latent), BF16),
            vmem((halo, latent), BF16),
            vmem((halo, latent), BF16),
            vmem((6, QUART, half), BF16),
            vmem((6, QUART, half), BF16),
            pltpu.SemaphoreType.DMA((len(operands),)),
            pltpu.SemaphoreType.DMA((neighbours,)),
            pltpu.SemaphoreType.DMA((neighbours,)),
            pltpu.SemaphoreType.DMA((neighbours,)),
            pltpu.SemaphoreType.DMA((neighbours,)),
            pltpu.SemaphoreType.DMA((6,)),
            pltpu.SemaphoreType.DMA((6,)),
        ],
        compiler_params=pltpu.CompilerParams(
            collective_id=0, has_side_effects=True, vmem_limit_bytes=60 * 1024 * 1024
        ),
        cost_estimate=pl.CostEstimate(
            flops=2 * 1000 * 1000 * 1000, bytes_accessed=4 * 1024 * 1024, transcendentals=0
        ),
    )(*operands)


def solution(mesh):
    return jax.shard_map(
        per_device,
        mesh=mesh,
        in_specs=(
            P("sec", "tile", None),
            P("sec", "tile", None),
            P("sec", "tile"),
            P("sec", "tile"),
            P("sec", "tile"),
            P("sec", "tile", None),
            P("sec", "tile", None),
            P("sec", "tile"),
            P("sec", "tile"),
            P(),
            P(),
        ),
        out_specs=P("sec", "tile", None),
        check_vma=False,
    )
```

```python
import functools

import jax
import jax.numpy as jnp
from jax import lax
from jax.experimental import pallas as pl
from jax.experimental.pallas import tpu as pltpu
from jax.sharding import PartitionSpec as P

MESH = pl.DeviceIdType.MESH
QUART = 128
GROUP = 4
NT = (((1,), (1,)), ((), ()))
F32 = jnp.float32
BF16 = jnp.bfloat16


def offset_value(number, neighbours):
    half = neighbours // 2
    return number - half + 1 if number >= half else number - half


def iota(shape, dim):
    return lax.broadcasted_iota(jnp.int32, shape, dim)


def hot(mask):
    return jnp.where(mask, F32(1.0), F32(0.0)).astype(BF16)


def dot(a, b):
    return jnp.dot(a, b, preferred_element_type=F32)


def dot_nt(a, b):
    return lax.dot_general(a, b, NT, preferred_element_type=F32)


def split_bf16(x):
    high = x.astype(BF16)
    return high, (x - high.astype(F32)).astype(BF16)


def kernel(
    sec_count,
    tile_count,
    neighbours,
    pre_hbm,
    cot_hbm,
    recv_hbm,
    slot_hbm,
    ecnt_smem,
    hmap_hbm,
    dec_hbm,
    dcnt_hbm,
    dnode_hbm,
    wnode_hbm,
    wout_hbm,
    out_ref,
    pre,
    cot,
    recv,
    slot,
    hmaps,
    dec,
    dcnt,
    dnode,
    wnode,
    wout,
    edge_proj,
    slope,
    delta,
    hot_edge,
    hot_sums,
    hot_dec,
    hot_land,
    node_split,
    node_cot,
    base,
    sums,
    dec_out,
    dec_in,
    halo_out,
    halo_in,
    local_out,
    local_in,
    landed_out,
    landed_in,
    load_sem,
    map_send,
    map_recv,
    dec_sem,
    halo_sem,
    local_send,
    local_recv,
    landed_send,
    landed_recv,
):
    edges, latent = cot.shape
    rows = dec.shape[0]
    groups = dec_in.shape[0]
    block = groups // neighbours
    capacity = rows // neighbours
    width = latent // sec_count
    local_rows = sec_count * QUART
    sec = lax.axis_index("sec")
    tile = lax.axis_index("tile")
    others = [lax.rem(sec + k, sec_count) for k in range(sec_count)]
    peers = [
        lax.rem(tile + offset_value(o, neighbours) + tile_count, tile_count)
        for o in range(neighbours)
    ]
    far_first = sorted(range(neighbours), key=lambda o: -abs(offset_value(o, neighbours)))

    def load(i, src, dst):
        return pltpu.make_async_copy(src, dst, load_sem.at[i])

    first_loads = [load(0, dcnt_hbm, dcnt), load(1, dec_hbm.at[0], dec)]
    edge_loads = [
        load(2, cot_hbm.at[0], cot),
        load(3, wout_hbm, wout),
        load(4, pre_hbm.at[0], pre),
    ]
    index_loads = [
        load(5, recv_hbm, recv),
        load(6, slot_hbm, slot),
        load(7, dnode_hbm, dnode),
        load(8, hmap_hbm.at[0], hmaps.at[sec]),
    ]
    weight_load = load(9, wnode_hbm, wnode)
    for copy in first_loads:
        copy.start()

    barrier = pltpu.get_barrier_semaphore()
    for o in far_first:
        pl.semaphore_signal(barrier, inc=1, device_id=(sec, peers[o]), device_id_type=MESH)
    for other in others[1:]:
        pl.semaphore_signal(barrier, inc=1, device_id=(other, tile), device_id_type=MESH)

    for copy in edge_loads + index_loads + [weight_load]:
        copy.start()

    def over_sec(k, src, dst, send_sem, recv_sem):
        return pltpu.make_async_remote_copy(
            src_ref=src,
            dst_ref=dst,
            send_sem=send_sem.at[k - 1],
            recv_sem=recv_sem.at[k - 1],
            device_id=(others[k], tile),
            device_id_type=MESH,
        )

    def over_tile(o, quarter, src, dst, sem):
        return pltpu.make_async_remote_copy(
            src_ref=src,
            dst_ref=dst,
            send_sem=sem.at[0],
            recv_sem=sem.at[1],
            device_id=(quarter, peers[o]),
            device_id_type=MESH,
        )

    first_loads[0].wait()
    lane = iota((1, rows), 1)
    count = jnp.zeros((1, rows), jnp.int32)
    for o in range(neighbours):
        count = jnp.where(lane // capacity == o, dcnt[0:1, o : o + 1], count)
    live_lane = jnp.where(lane % capacity < count, lane // GROUP, -1)
    pick = hot(iota((groups, rows), 0) == live_lane)
    first_loads[1].wait()
    dec_out[...] = dot(pick, dec[...]).astype(BF16)

    pl.semaphore_wait(barrier, neighbours + sec_count - 1)

    for o in far_first:
        at = pl.ds(o * block, block)
        over_tile(o, sec, dec_out.at[at], dec_in.at[at], dec_sem).start()
    map_copies = [
        over_sec(k, hmap_hbm.at[0], hmaps.at[sec], map_send, map_recv)
        for k in range(1, sec_count)
    ]
    for copy in map_copies:
        copy.start()

    for copy in edge_loads:
        copy.wait()
    step = 256

    def edge_block(i, carry):
        at = pl.ds(i * step, step)
        edge_proj[at, :] = dot_nt(cot[at, :], wout[...])
        v = pre[at, :].astype(F32)
        s = jax.nn.sigmoid(v)
        slope[at, :] = s * (1.0 + v * (1.0 - s))
        return carry

    lax.fori_loop(0, edges // step, edge_block, 0)

    for copy in index_loads:
        copy.wait()
    node_row = iota((QUART, edges), 0)
    receivers = recv[...]
    edge_hot = jnp.where(node_row == receivers, F32(1.0), F32(0.0)).T.astype(BF16)
    hot_edge[:, :QUART] = edge_hot
    hot_edge[:, QUART:] = edge_hot
    live = iota((1, edges), 1) < ecnt_smem[0, 0]
    live_slot = jnp.where(live, slot[...], -1)
    live_recv = jnp.where(live, receivers, -1)
    hot_sums[0:QUART, :] = hot(node_row == live_slot - local_rows)
    for k in range(sec_count):
        hot_sums[(k + 1) * QUART : (k + 2) * QUART, :] = hot(
            node_row == live_slot - others[k] * QUART
        )
    hot_sums[(sec_count + 1) * QUART :, :] = hot(node_row == live_recv)
    first_of_group = jnp.where(lane % GROUP == 0, dnode[...], -1)
    named = hot(iota((QUART, rows), 0) == first_of_group)
    group_of = hot(iota((groups, rows), 0) == lane // GROUP)
    hot_dec[...] = dot_nt(named, group_of).astype(BF16)

    pltpu.make_async_copy(dec_in, dec_in, dec_sem.at[1]).wait()
    cot_sum = dot(hot_dec[...], dec_in[...])
    node_cot[...] = cot_sum
    high, low = split_bf16(dot_nt(cot_sum.astype(BF16), wout[...]))
    node_split[:QUART, :] = high
    node_split[QUART:, :] = low

    def delta_block(i, carry):
        at = pl.ds(i * step, step)
        act = edge_proj[at, :] + dot(hot_edge[at, :], node_split[...])
        delta[at, :] = (act * slope[at, :]).astype(BF16)
        return carry

    lax.fori_loop(0, edges // step, delta_block, 0)

    halo_rows = dot(hot_sums[0:QUART, :], delta[...]).astype(BF16)
    for j in range(sec_count):
        halo_out[j] = halo_rows[:, j * width : (j + 1) * width]
    for o in far_first:
        at = pl.ds(o * block, block)
        for j in range(sec_count):
            over_tile(o, j, halo_out.at[j, at], halo_in.at[sec, at], halo_sem).start()

    def sum_block(i, carry):
        at = pl.ds(i * QUART, QUART)
        sums[at, :] = dot(hot_sums[pl.ds((i + 1) * QUART, QUART), :], delta[...])
        return carry

    lax.fori_loop(1, sec_count, sum_block, 0)
    local_copies = [
        over_sec(k, local_out.at[k - 1], local_in.at[k - 1], local_send, local_recv)
        for k in range(1, sec_count)
    ]
    for k in range(1, sec_count):
        local_out[k - 1] = sums[k * QUART : (k + 1) * QUART, :].astype(BF16)
        local_copies[k - 1].start()
    sum_block(0, 0)
    sum_block(sec_count, 0)

    for copy in map_copies:
        copy.wait_recv()
    for k in range(sec_count):
        for q in range(sec_count):
            hot_land[k * QUART : (k + 1) * QUART, q * QUART : (q + 1) * QUART] = hot(
                iota((QUART, QUART), 0) == hmaps[q] - others[k] * QUART
            )
    weight_load.wait()
    received = split_bf16(sums[sec_count * QUART :, :])
    base[...] = (
        node_cot[...]
        + dot_nt(received[0], wnode[latent:, :])
        + dot_nt(received[1], wnode[latent:, :])
    )

    pltpu.make_async_copy(halo_in, halo_in, halo_sem.at[1]).wait()
    arrived = halo_in[...].reshape(local_rows, width)
    landed = dot(hot_land[...], arrived).astype(BF16)
    landed_copies = [
        over_sec(k, landed_out.at[k - 1], landed_in.at[sec], landed_send, landed_recv)
        for k in range(1, sec_count)
    ]
    for k in range(1, sec_count):
        landed_out[k - 1] = landed[k * QUART : (k + 1) * QUART, :]
    for copy in landed_copies:
        copy.start()
    landed_in[sec] = landed[:QUART, :]

    own = sums[:QUART, :]
    for k in range(1, sec_count):
        local_copies[k - 1].wait_recv()
        own += local_in[k - 1].astype(F32)
    sent = split_bf16(own)
    base[...] += dot_nt(sent[0], wnode[:latent, :]) + dot_nt(sent[1], wnode[:latent, :])

    for copy in landed_copies:
        copy.wait_recv()
    result = base[...]
    for j in range(sec_count):
        result += dot_nt(landed_in[j], wnode[:latent, j * width : (j + 1) * width])
    out_ref[0] = result

    for copy in map_copies + local_copies + landed_copies:
        copy.wait_send()
    pltpu.make_async_copy(dec_out, dec_out, dec_sem.at[0]).wait()
    pltpu.make_async_copy(halo_out, halo_out, halo_sem.at[0]).wait()


def per_device(
    pre_act,
    edge_cot,
    recv_local,
    send_slot,
    edge_count,
    halo_map,
    dec_rows,
    dec_count,
    dec_node,
    w_node,
    w_out,
):
    sec_count = lax.axis_size("sec")
    tile_count = lax.axis_size("tile")
    edges, latent = pre_act.shape[1:]
    rows = dec_rows.shape[1]
    neighbours = dec_count.shape[1]
    groups = rows // GROUP
    halo = halo_map.shape[2]
    width = latent // sec_count
    def hbm(x):
        return pltpu.with_memory_space_constraint(x, pltpu.HBM)

    operands = (
        hbm(pre_act),
        hbm(edge_cot),
        hbm(recv_local),
        hbm(send_slot),
        edge_count,
        hbm(halo_map),
        hbm(dec_rows),
        hbm(dec_count),
        hbm(dec_node),
        hbm(w_node),
        hbm(w_out),
    )
    vmem = pltpu.VMEM
    dma = pltpu.SemaphoreType.DMA
    return pl.pallas_call(
        functools.partial(kernel, sec_count, tile_count, neighbours),
        out_shape=vmem((1, QUART, latent), F32),
        in_specs=[
            pl.BlockSpec(memory_space=pltpu.SMEM if x is edge_count else pl.ANY) for x in operands
        ],
        out_specs=pl.BlockSpec(memory_space=vmem),
        scratch_shapes=[
            vmem((edges, latent), BF16),
            vmem((edges, latent), BF16),
            vmem((1, edges), jnp.int32),
            vmem((1, edges), jnp.int32),
            vmem((sec_count, 1, halo), jnp.int32),
            vmem((rows, latent), BF16),
            vmem((1, neighbours), jnp.int32),
            vmem((1, rows), jnp.int32),
            vmem(w_node.shape, BF16),
            vmem(w_out.shape, BF16),
            vmem((edges, latent), F32),
            vmem((edges, latent), F32),
            vmem((edges, latent), BF16),
            vmem((edges, 2 * QUART), BF16),
            vmem(((sec_count + 2) * QUART, edges), BF16),
            vmem((QUART, groups), BF16),
            vmem((sec_count * QUART, sec_count * halo), BF16),
            vmem((2 * QUART, latent), BF16),
            vmem((QUART, latent), F32),
            vmem((QUART, latent), F32),
            vmem(((sec_count + 1) * QUART, latent), F32),
            vmem((groups, latent), BF16),
            vmem((groups, latent), BF16),
            vmem((sec_count, halo, width), BF16),
            vmem((sec_count, halo, width), BF16),
            vmem((sec_count - 1, QUART, latent), BF16),
            vmem((sec_count - 1, QUART, latent), BF16),
            vmem((sec_count - 1, QUART, width), BF16),
            vmem((sec_count, QUART, width), BF16),
            dma((10,)),
            dma((sec_count - 1,)),
            dma((sec_count - 1,)),
            dma((2,)),
            dma((2,)),
            dma((sec_count - 1,)),
            dma((sec_count - 1,)),
            dma((sec_count - 1,)),
            dma((sec_count - 1,)),
        ],
        compiler_params=pltpu.CompilerParams(
            collective_id=0, has_side_effects=True, vmem_limit_bytes=40 * 1024 * 1024
        ),
        cost_estimate=pl.CostEstimate(
            flops=2 * 1000 * 1000 * 1000, bytes_accessed=4 * 1024 * 1024, transcendentals=0
        ),
    )(*operands)


def solution(mesh):
    return jax.shard_map(
        per_device,
        mesh=mesh,
        in_specs=(
            P("sec", "tile", None),
            P("sec", "tile", None),
            P("sec", "tile"),
            P("sec", "tile"),
            P("sec", "tile"),
            P("sec", "tile", None),
            P("sec", "tile", None),
            P("sec", "tile"),
            P("sec", "tile"),
            P(),
            P(),
        ),
        out_specs=P("sec", "tile", None),
        check_vma=False,
    )
```

```python
import functools

import jax
import jax.numpy as jnp
from jax import lax
from jax.experimental import pallas as pl
from jax.experimental.pallas import tpu as pltpu
from jax.sharding import PartitionSpec as P

MESH = pl.DeviceIdType.MESH
QUART = 128
GROUP = 4
PAIR = 4
NT = (((1,), (1,)), ((), ()))
F32 = jnp.float32
BF16 = jnp.bfloat16


def offset_value(number, neighbours):
    half = neighbours // 2
    return number - half + 1 if number >= half else number - half


def iota(shape, dim):
    return lax.broadcasted_iota(jnp.int32, shape, dim)


def hot(mask):
    return jnp.where(mask, F32(1.0), F32(0.0)).astype(BF16)


def dot(a, b):
    return jnp.dot(a, b, preferred_element_type=F32)


def dot_nt(a, b):
    return lax.dot_general(a, b, NT, preferred_element_type=F32)


def split_bf16(x):
    high = x.astype(BF16)
    return high, (x - high.astype(F32)).astype(BF16)


def kernel(
    sec_count,
    tile_count,
    neighbours,
    pre_hbm,
    cot_hbm,
    recv_hbm,
    slot_hbm,
    ecnt_smem,
    hmap_hbm,
    dec_hbm,
    dcnt_hbm,
    dnode_hbm,
    wnode_hbm,
    wout_hbm,
    out_ref,
    pre,
    cot,
    recv,
    slot,
    hmaps,
    dec,
    dcnt,
    dnode,
    wnode,
    wout,
    edge_proj,
    slope,
    delta,
    hot_edge,
    hot_sums,
    hot_dec,
    hot_land,
    node_split,
    node_cot,
    base,
    sums,
    dec_out,
    dec_in,
    halo_out,
    halo_in,
    local_out,
    local_in,
    landed_out,
    landed_in,
    load_sem,
    map_send,
    map_recv,
    dec_sem,
    halo_sem,
    local_send,
    local_recv,
    landed_send,
    landed_recv,
):
    edges, latent = cot.shape
    rows = dec.shape[0]
    groups = dec_in.shape[0]
    block = groups // neighbours
    capacity = rows // neighbours
    width = latent // PAIR
    local_rows = sec_count * QUART
    sec = lax.axis_index("sec")
    tile = lax.axis_index("tile")
    others = [lax.rem(sec + k, sec_count) for k in range(sec_count)]
    peers = [
        lax.rem(tile + offset_value(o, neighbours) + tile_count, tile_count)
        for o in range(neighbours)
    ]
    far_first = sorted(range(neighbours), key=lambda o: -abs(offset_value(o, neighbours)))

    far_pairs = sorted(
        ((o, k) for o in range(neighbours) for k in range(sec_count)),
        key=lambda pair: -(
            abs(offset_value(pair[0], neighbours)) / 2 + min(pair[1], sec_count - pair[1])
        ),
    )

    def load(i, src, dst):
        return pltpu.make_async_copy(src, dst, load_sem.at[i])

    first_loads = [load(0, dcnt_hbm, dcnt), load(1, dec_hbm.at[0], dec)]
    edge_loads = [
        load(2, cot_hbm.at[0], cot),
        load(3, wout_hbm, wout),
        load(4, pre_hbm.at[0], pre),
    ]
    index_loads = [
        load(5, recv_hbm, recv),
        load(6, slot_hbm, slot),
        load(7, dnode_hbm, dnode),
        load(8, hmap_hbm.at[0], hmaps.at[sec]),
    ]
    weight_load = load(9, wnode_hbm, wnode)
    for copy in first_loads:
        copy.start()

    barrier = pltpu.get_barrier_semaphore()
    for o in far_first:
        pl.semaphore_signal(barrier, inc=1, device_id=(sec, peers[o]), device_id_type=MESH)
    for other in others[1:]:
        pl.semaphore_signal(barrier, inc=1, device_id=(other, tile), device_id_type=MESH)

    for copy in edge_loads + index_loads + [weight_load]:
        copy.start()

    def over_sec(k, src, dst, send_sem, recv_sem):
        return pltpu.make_async_remote_copy(
            src_ref=src,
            dst_ref=dst,
            send_sem=send_sem.at[k - 1],
            recv_sem=recv_sem.at[k - 1],
            device_id=(others[k], tile),
            device_id_type=MESH,
        )

    def over_tile(o, quarter, src, dst, sem):
        return pltpu.make_async_remote_copy(
            src_ref=src,
            dst_ref=dst,
            send_sem=sem.at[0],
            recv_sem=sem.at[1],
            device_id=(quarter, peers[o]),
            device_id_type=MESH,
        )

    first_loads[0].wait()
    lane = iota((1, rows), 1)
    count = jnp.zeros((1, rows), jnp.int32)
    for o in range(neighbours):
        count = jnp.where(lane // capacity == o, dcnt[0:1, o : o + 1], count)
    live_lane = jnp.where(lane % capacity < count, lane // GROUP, -1)
    pick = hot(iota((groups, rows), 0) == live_lane)
    first_loads[1].wait()
    dec_out[...] = dot(pick, dec[...]).astype(BF16)

    pl.semaphore_wait(barrier, neighbours + sec_count - 1)

    for o in far_first:
        at = pl.ds(o * block, block)
        over_tile(o, sec, dec_out.at[at], dec_in.at[at], dec_sem).start()
    map_copies = [
        over_sec(k, hmap_hbm.at[0], hmaps.at[sec], map_send, map_recv)
        for k in range(1, sec_count)
    ]
    for copy in map_copies:
        copy.start()

    for copy in edge_loads:
        copy.wait()
    step = 256

    def edge_block(i, carry):
        at = pl.ds(i * step, step)
        edge_proj[at, :] = dot_nt(cot[at, :], wout[...])
        v = pre[at, :].astype(F32)
        s = jax.nn.sigmoid(v)
        slope[at, :] = s * (1.0 + v * (1.0 - s))
        return carry

    lax.fori_loop(0, edges // step, edge_block, 0)

    for copy in index_loads:
        copy.wait()
    node_row = iota((QUART, edges), 0)
    receivers = recv[...]
    edge_hot = jnp.where(node_row == receivers, F32(1.0), F32(0.0)).T.astype(BF16)
    hot_edge[:, :QUART] = edge_hot
    hot_edge[:, QUART:] = edge_hot
    live = iota((1, edges), 1) < ecnt_smem[0, 0]
    live_slot = jnp.where(live, slot[...], -1)
    live_recv = jnp.where(live, receivers, -1)
    hot_sums[0:QUART, :] = hot(node_row == live_slot - local_rows)
    for k in range(sec_count):
        hot_sums[(k + 1) * QUART : (k + 2) * QUART, :] = hot(
            node_row == live_slot - others[k] * QUART
        )
    hot_sums[(sec_count + 1) * QUART :, :] = hot(node_row == live_recv)
    first_of_group = jnp.where(lane % GROUP == 0, dnode[...], -1)
    named = hot(iota((QUART, rows), 0) == first_of_group)
    group_of = hot(iota((groups, rows), 0) == lane // GROUP)
    hot_dec[...] = dot_nt(named, group_of).astype(BF16)

    pltpu.make_async_copy(dec_in, dec_in, dec_sem.at[1]).wait()
    cot_sum = dot(hot_dec[...], dec_in[...])
    node_cot[...] = cot_sum
    high, low = split_bf16(dot_nt(cot_sum.astype(BF16), wout[...]))
    node_split[:QUART, :] = high
    node_split[QUART:, :] = low

    def delta_block(i, carry):
        at = pl.ds(i * step, step)
        act = edge_proj[at, :] + dot(hot_edge[at, :], node_split[...])
        delta[at, :] = (act * slope[at, :]).astype(BF16)
        return carry

    lax.fori_loop(0, edges // step, delta_block, 0, unroll=True)

    halo_rows = dot(hot_sums[0:QUART, :], delta[...]).astype(BF16)
    for j in range(PAIR):
        halo_out[j] = halo_rows[:, j * width : (j + 1) * width]
    for o, k in far_pairs:
        at = pl.ds(o * block, block)
        over_tile(
            o, others[k], halo_out.at[others[k], at], halo_in.at[sec, at], halo_sem
        ).start()

    def sum_block(i, carry):
        at = pl.ds(i * QUART, QUART)
        sums[at, :] = dot(hot_sums[pl.ds((i + 1) * QUART, QUART), :], delta[...])
        return carry

    lax.fori_loop(1, sec_count, sum_block, 0)
    local_copies = [
        over_sec(k, local_out.at[k - 1], local_in.at[k - 1], local_send, local_recv)
        for k in range(1, sec_count)
    ]
    for k in range(1, sec_count):
        local_out[k - 1] = sums[k * QUART : (k + 1) * QUART, :].astype(BF16)
        local_copies[k - 1].start()
    sum_block(0, 0)
    sum_block(sec_count, 0)

    for copy in map_copies:
        copy.wait_recv()
    for k in range(sec_count):
        for q in range(PAIR):
            hot_land[k * QUART : (k + 1) * QUART, q * QUART : (q + 1) * QUART] = hot(
                iota((QUART, QUART), 0) == hmaps[q] - others[k] * QUART
            )
    weight_load.wait()
    received = split_bf16(sums[sec_count * QUART :, :])
    base[...] = (
        node_cot[...]
        + dot_nt(received[0], wnode[latent:, :])
        + dot_nt(received[1], wnode[latent:, :])
    )

    pltpu.make_async_copy(halo_in, halo_in, halo_sem.at[1]).wait()
    arrived = halo_in[...].reshape(PAIR * QUART, width)
    landed = dot(hot_land[...], arrived).astype(BF16)
    landed_copies = [
        over_sec(k, landed_out.at[k - 1], landed_in.at[sec], landed_send, landed_recv)
        for k in range(1, sec_count)
    ]
    for k in range(1, sec_count):
        landed_out[k - 1] = landed[k * QUART : (k + 1) * QUART, :]
    for copy in landed_copies:
        copy.start()
    landed_in[sec] = landed[:QUART, :]

    total = sums[:QUART, :]
    for k in range(1, sec_count):
        local_copies[k - 1].wait_recv()
        total += local_in[k - 1].astype(F32)
    sent = split_bf16(total)
    base[...] += dot_nt(sent[0], wnode[:latent, :]) + dot_nt(sent[1], wnode[:latent, :])

    for copy in landed_copies:
        copy.wait_recv()
    columns = jnp.concatenate([landed_in[j] for j in range(sec_count)], axis=1)
    weights = jnp.concatenate([wnode[:latent, :]] * (sec_count // PAIR), axis=1)
    out_ref[0] = base[...] + dot_nt(columns, weights)

    for copy in map_copies + local_copies + landed_copies:
        copy.wait_send()
    pltpu.make_async_copy(dec_out, dec_out, dec_sem.at[0]).wait()
    pltpu.make_async_copy(halo_out, halo_out, halo_sem.at[0]).wait()


def per_device(
    pre_act,
    edge_cot,
    recv_local,
    send_slot,
    edge_count,
    halo_map,
    dec_rows,
    dec_count,
    dec_node,
    w_node,
    w_out,
):
    sec_count = lax.axis_size("sec")
    tile_count = lax.axis_size("tile")
    edges, latent = pre_act.shape[1:]
    rows = dec_rows.shape[1]
    neighbours = dec_count.shape[1]
    groups = rows // GROUP
    halo = halo_map.shape[2]
    width = latent // PAIR
    def hbm(x):
        return pltpu.with_memory_space_constraint(x, pltpu.HBM)

    operands = (
        hbm(pre_act),
        hbm(edge_cot),
        hbm(recv_local),
        hbm(send_slot),
        edge_count,
        hbm(halo_map),
        hbm(dec_rows),
        hbm(dec_count),
        hbm(dec_node),
        hbm(w_node),
        hbm(w_out),
    )
    vmem = pltpu.VMEM
    dma = pltpu.SemaphoreType.DMA
    return pl.pallas_call(
        functools.partial(kernel, sec_count, tile_count, neighbours),
        out_shape=vmem((1, QUART, latent), F32),
        in_specs=[
            pl.BlockSpec(memory_space=pltpu.SMEM if x is edge_count else pl.ANY) for x in operands
        ],
        out_specs=pl.BlockSpec(memory_space=vmem),
        scratch_shapes=[
            vmem((edges, latent), BF16),
            vmem((edges, latent), BF16),
            vmem((1, edges), jnp.int32),
            vmem((1, edges), jnp.int32),
            vmem((PAIR, 1, halo), jnp.int32),
            vmem((rows, latent), BF16),
            vmem((1, neighbours), jnp.int32),
            vmem((1, rows), jnp.int32),
            vmem(w_node.shape, BF16),
            vmem(w_out.shape, BF16),
            vmem((edges, latent), F32),
            vmem((edges, latent), F32),
            vmem((edges, latent), BF16),
            vmem((edges, 2 * QUART), BF16),
            vmem(((sec_count + 2) * QUART, edges), BF16),
            vmem((QUART, groups), BF16),
            vmem((sec_count * QUART, PAIR * halo), BF16),
            vmem((2 * QUART, latent), BF16),
            vmem((QUART, latent), F32),
            vmem((QUART, latent), F32),
            vmem(((sec_count + 1) * QUART, latent), F32),
            vmem((groups, latent), BF16),
            vmem((groups, latent), BF16),
            vmem((PAIR, halo, width), BF16),
            vmem((PAIR, halo, width), BF16),
            vmem((sec_count - 1, QUART, latent), BF16),
            vmem((sec_count - 1, QUART, latent), BF16),
            vmem((sec_count - 1, QUART, width), BF16),
            vmem((sec_count, QUART, width), BF16),
            dma((10,)),
            dma((sec_count - 1,)),
            dma((sec_count - 1,)),
            dma((2,)),
            dma((2,)),
            dma((sec_count - 1,)),
            dma((sec_count - 1,)),
            dma((sec_count - 1,)),
            dma((sec_count - 1,)),
        ],
        compiler_params=pltpu.CompilerParams(
            collective_id=0, has_side_effects=True, vmem_limit_bytes=40 * 1024 * 1024
        ),
        cost_estimate=pl.CostEstimate(
            flops=2 * 1000 * 1000 * 1000, bytes_accessed=4 * 1024 * 1024, transcendentals=0
        ),
    )(*operands)


def solution(mesh):
    return jax.shard_map(
        per_device,
        mesh=mesh,
        in_specs=(
            P("sec", "tile", None),
            P("sec", "tile", None),
            P("sec", "tile"),
            P("sec", "tile"),
            P("sec", "tile"),
            P("sec", "tile", None),
            P("sec", "tile", None),
            P("sec", "tile"),
            P("sec", "tile"),
            P(),
            P(),
        ),
        out_specs=P("sec", "tile", None),
        check_vma=False,
    )
```

```python
import functools

import jax
import jax.numpy as jnp
from jax import lax
from jax.experimental import pallas as pl
from jax.experimental.pallas import tpu as pltpu
from jax.sharding import PartitionSpec as P

MESH = pl.DeviceIdType.MESH
QUART = 128
GROUP = 4
PAIR = 4
NT = (((1,), (1,)), ((), ()))
F32 = jnp.float32
BF16 = jnp.bfloat16


def offset_value(number, neighbours):
    half = neighbours // 2
    return number - half + 1 if number >= half else number - half


def iota(shape, dim):
    return lax.broadcasted_iota(jnp.int32, shape, dim)


def hot(mask):
    return jnp.where(mask, F32(1.0), F32(0.0)).astype(BF16)


def dot(a, b):
    return jnp.dot(a, b, preferred_element_type=F32)


def dot_nt(a, b):
    return lax.dot_general(a, b, NT, preferred_element_type=F32)


def split_bf16(x):
    high = x.astype(BF16)
    return high, (x - high.astype(F32)).astype(BF16)


def kernel(
    sec_count,
    tile_count,
    neighbours,
    pre_hbm,
    cot_hbm,
    recv_hbm,
    slot_hbm,
    ecnt_smem,
    hmap_hbm,
    dec_hbm,
    dcnt_hbm,
    dnode_hbm,
    wnode_hbm,
    wout_hbm,
    out_ref,
    pre,
    cot,
    recv,
    slot,
    hmaps,
    dec,
    dcnt,
    dnode,
    wnode,
    wout,
    wout_t,
    wsend_t,
    edge_proj,
    slope,
    delta,
    hot_edge,
    hot_sums,
    hot_dec,
    hot_land,
    node_split,
    node_cot,
    base,
    sums,
    dec_out,
    dec_in,
    halo_out,
    halo_in,
    local_out,
    local_in,
    landed_out,
    landed_in,
    load_sem,
    map_send,
    map_recv,
    dec_sem,
    halo_sem,
    local_send,
    local_recv,
    landed_send,
    landed_recv,
):
    edges, latent = cot.shape
    rows = dec.shape[0]
    groups = dec_in.shape[0]
    block = groups // neighbours
    capacity = rows // neighbours
    width = latent // PAIR
    local_rows = sec_count * QUART
    sec = lax.axis_index("sec")
    tile = lax.axis_index("tile")
    others = [lax.rem(sec + k, sec_count) for k in range(sec_count)]
    peers = [
        lax.rem(tile + offset_value(o, neighbours) + tile_count, tile_count)
        for o in range(neighbours)
    ]
    far_first = sorted(range(neighbours), key=lambda o: -abs(offset_value(o, neighbours)))

    far_pairs = sorted(
        ((o, k) for o in range(neighbours) for k in range(sec_count)),
        key=lambda pair: -(
            abs(offset_value(pair[0], neighbours)) / 2 + min(pair[1], sec_count - pair[1])
        ),
    )

    def load(i, src, dst):
        return pltpu.make_async_copy(src, dst, load_sem.at[i])

    first_loads = [load(0, dcnt_hbm, dcnt), load(1, dec_hbm.at[0], dec)]
    edge_loads = [
        load(2, cot_hbm.at[0], cot),
        load(3, wout_hbm, wout),
        load(4, pre_hbm.at[0], pre),
    ]
    index_loads = [
        load(5, recv_hbm, recv),
        load(6, slot_hbm, slot),
        load(7, dnode_hbm, dnode),
        load(8, hmap_hbm.at[0], hmaps.at[sec]),
    ]
    weight_load = load(9, wnode_hbm, wnode)
    for copy in first_loads:
        copy.start()

    barrier = pltpu.get_barrier_semaphore()
    for o in far_first:
        pl.semaphore_signal(barrier, inc=1, device_id=(sec, peers[o]), device_id_type=MESH)
    for other in others[1:]:
        pl.semaphore_signal(barrier, inc=1, device_id=(other, tile), device_id_type=MESH)

    for copy in edge_loads + index_loads + [weight_load]:
        copy.start()

    def over_sec(k, src, dst, send_sem, recv_sem):
        return pltpu.make_async_remote_copy(
            src_ref=src,
            dst_ref=dst,
            send_sem=send_sem.at[k - 1],
            recv_sem=recv_sem.at[k - 1],
            device_id=(others[k], tile),
            device_id_type=MESH,
        )

    def over_tile(o, quarter, src, dst, sem):
        return pltpu.make_async_remote_copy(
            src_ref=src,
            dst_ref=dst,
            send_sem=sem.at[0],
            recv_sem=sem.at[1],
            device_id=(quarter, peers[o]),
            device_id_type=MESH,
        )

    first_loads[0].wait()
    lane = iota((1, rows), 1)
    count = jnp.zeros((1, rows), jnp.int32)
    for o in range(neighbours):
        count = jnp.where(lane // capacity == o, dcnt[0:1, o : o + 1], count)
    live_lane = jnp.where(lane % capacity < count, lane // GROUP, -1)
    pick = hot(iota((groups, rows), 0) == live_lane)
    first_loads[1].wait()
    dec_out[...] = dot(pick, dec[...]).astype(BF16)

    pl.semaphore_wait(barrier, neighbours + sec_count - 1)

    for o in far_first:
        at = pl.ds(o * block, block)
        over_tile(o, sec, dec_out.at[at], dec_in.at[at], dec_sem).start()
    map_copies = [
        over_sec(k, hmap_hbm.at[0], hmaps.at[sec], map_send, map_recv)
        for k in range(1, sec_count)
    ]
    for copy in map_copies:
        copy.start()

    for copy in edge_loads:
        copy.wait()
    step = 256

    def edge_block(i, carry):
        at = pl.ds(i * step, step)
        edge_proj[at, :] = dot_nt(cot[at, :], wout[...])
        v = pre[at, :].astype(F32)
        s = jax.nn.sigmoid(v)
        slope[at, :] = s * (1.0 + v * (1.0 - s))
        return carry

    lax.fori_loop(0, edges // step, edge_block, 0)

    wout_t[...] = wout[...].astype(F32).T.astype(BF16)
    for copy in index_loads:
        copy.wait()
    node_row = iota((QUART, edges), 0)
    receivers = recv[...]
    edge_hot = jnp.where(node_row == receivers, F32(1.0), F32(0.0)).T.astype(BF16)
    hot_edge[:, :QUART] = edge_hot
    hot_edge[:, QUART:] = edge_hot
    live = iota((1, edges), 1) < ecnt_smem[0, 0]
    live_slot = jnp.where(live, slot[...], -1)
    live_recv = jnp.where(live, receivers, -1)
    hot_sums[0:QUART, :] = hot(node_row == live_slot - local_rows)
    for k in range(sec_count):
        hot_sums[(k + 1) * QUART : (k + 2) * QUART, :] = hot(
            node_row == live_slot - others[k] * QUART
        )
    hot_sums[(sec_count + 1) * QUART :, :] = hot(node_row == live_recv)
    first_of_group = jnp.where(lane % GROUP == 0, dnode[...], -1)
    named = hot(iota((QUART, rows), 0) == first_of_group)
    group_of = hot(iota((groups, rows), 0) == lane // GROUP)
    hot_dec[...] = dot_nt(named, group_of).astype(BF16)

    pltpu.make_async_copy(dec_in, dec_in, dec_sem.at[1]).wait()
    cot_sum = dot(hot_dec[...], dec_in[...])
    node_cot[...] = cot_sum
    high, low = split_bf16(dot(cot_sum.astype(BF16), wout_t[...]))
    node_split[:QUART, :] = high
    node_split[QUART:, :] = low

    def delta_block(i, carry):
        at = pl.ds(i * step, step)
        act = edge_proj[at, :] + dot(hot_edge[at, :], node_split[...])
        delta[at, :] = (act * slope[at, :]).astype(BF16)
        return carry

    lax.fori_loop(0, edges // step, delta_block, 0, unroll=True)

    halo_rows = dot(hot_sums[0:QUART, :], delta[...]).astype(BF16)
    for j in range(PAIR):
        halo_out[j] = halo_rows[:, j * width : (j + 1) * width]
    for o, k in far_pairs:
        at = pl.ds(o * block, block)
        over_tile(
            o, others[k], halo_out.at[others[k], at], halo_in.at[sec, at], halo_sem
        ).start()

    def sum_block(i, carry):
        at = pl.ds(i * QUART, QUART)
        sums[at, :] = dot(hot_sums[pl.ds((i + 1) * QUART, QUART), :], delta[...])
        return carry

    lax.fori_loop(1, sec_count, sum_block, 0)
    local_copies = [
        over_sec(k, local_out.at[k - 1], local_in.at[k - 1], local_send, local_recv)
        for k in range(1, sec_count)
    ]
    for k in range(1, sec_count):
        local_out[k - 1] = sums[k * QUART : (k + 1) * QUART, :].astype(BF16)
        local_copies[k - 1].start()
    sum_block(0, 0)
    sum_block(sec_count, 0)

    for copy in map_copies:
        copy.wait_recv()
    for k in range(sec_count):
        for q in range(PAIR):
            hot_land[k * QUART : (k + 1) * QUART, q * QUART : (q + 1) * QUART] = hot(
                iota((QUART, QUART), 0) == hmaps[q] - others[k] * QUART
            )
    weight_load.wait()
    wsend_t[...] = wnode[:latent, :].astype(F32).T.astype(BF16)
    received = split_bf16(sums[sec_count * QUART :, :])
    base[...] = (
        node_cot[...]
        + dot_nt(received[0], wnode[latent:, :])
        + dot_nt(received[1], wnode[latent:, :])
    )

    pltpu.make_async_copy(halo_in, halo_in, halo_sem.at[1]).wait()
    arrived = halo_in[...].reshape(PAIR * QUART, width)
    landed = dot(hot_land[...], arrived).astype(BF16)
    landed_copies = [
        over_sec(k, landed_out.at[k - 1], landed_in.at[sec], landed_send, landed_recv)
        for k in range(1, sec_count)
    ]
    for k in range(1, sec_count):
        landed_out[k - 1] = landed[k * QUART : (k + 1) * QUART, :]
    for copy in landed_copies:
        copy.start()
    landed_in[sec] = landed[:QUART, :]

    total = sums[:QUART, :]
    for k in range(1, sec_count):
        local_copies[k - 1].wait_recv()
        total += local_in[k - 1].astype(F32)
    sent = split_bf16(total)
    base[...] += dot_nt(sent[0], wnode[:latent, :]) + dot_nt(sent[1], wnode[:latent, :])

    for copy in landed_copies:
        copy.wait_recv()
    columns = jnp.concatenate([landed_in[j] for j in range(sec_count)], axis=1)
    out_ref[0] = base[...] + dot(columns, wsend_t[...])

    for copy in map_copies + local_copies + landed_copies:
        copy.wait_send()
    pltpu.make_async_copy(dec_out, dec_out, dec_sem.at[0]).wait()
    pltpu.make_async_copy(halo_out, halo_out, halo_sem.at[0]).wait()


def per_device(
    pre_act,
    edge_cot,
    recv_local,
    send_slot,
    edge_count,
    halo_map,
    dec_rows,
    dec_count,
    dec_node,
    w_node,
    w_out,
):
    sec_count = lax.axis_size("sec")
    tile_count = lax.axis_size("tile")
    edges, latent = pre_act.shape[1:]
    rows = dec_rows.shape[1]
    neighbours = dec_count.shape[1]
    groups = rows // GROUP
    halo = halo_map.shape[2]
    width = latent // PAIR
    def hbm(x):
        return pltpu.with_memory_space_constraint(x, pltpu.HBM)

    operands = (
        hbm(pre_act),
        hbm(edge_cot),
        hbm(recv_local),
        hbm(send_slot),
        edge_count,
        hbm(halo_map),
        hbm(dec_rows),
        hbm(dec_count),
        hbm(dec_node),
        hbm(w_node),
        hbm(w_out),
    )
    vmem = pltpu.VMEM
    dma = pltpu.SemaphoreType.DMA
    return pl.pallas_call(
        functools.partial(kernel, sec_count, tile_count, neighbours),
        out_shape=vmem((1, QUART, latent), F32),
        in_specs=[
            pl.BlockSpec(memory_space=pltpu.SMEM if x is edge_count else pl.ANY) for x in operands
        ],
        out_specs=pl.BlockSpec(memory_space=vmem),
        scratch_shapes=[
            vmem((edges, latent), BF16),
            vmem((edges, latent), BF16),
            vmem((1, edges), jnp.int32),
            vmem((1, edges), jnp.int32),
            vmem((PAIR, 1, halo), jnp.int32),
            vmem((rows, latent), BF16),
            vmem((1, neighbours), jnp.int32),
            vmem((1, rows), jnp.int32),
            vmem(w_node.shape, BF16),
            vmem(w_out.shape, BF16),
            vmem((latent, latent), BF16),
            vmem((latent, latent), BF16),
            vmem((edges, latent), F32),
            vmem((edges, latent), F32),
            vmem((edges, latent), BF16),
            vmem((edges, 2 * QUART), BF16),
            vmem(((sec_count + 2) * QUART, edges), BF16),
            vmem((QUART, groups), BF16),
            vmem((sec_count * QUART, PAIR * halo), BF16),
            vmem((2 * QUART, latent), BF16),
            vmem((QUART, latent), F32),
            vmem((QUART, latent), F32),
            vmem(((sec_count + 1) * QUART, latent), F32),
            vmem((groups, latent), BF16),
            vmem((groups, latent), BF16),
            vmem((PAIR, halo, width), BF16),
            vmem((PAIR, halo, width), BF16),
            vmem((sec_count - 1, QUART, latent), BF16),
            vmem((sec_count - 1, QUART, latent), BF16),
            vmem((sec_count - 1, QUART, width), BF16),
            vmem((sec_count, QUART, width), BF16),
            dma((10,)),
            dma((sec_count - 1,)),
            dma((sec_count - 1,)),
            dma((2,)),
            dma((2,)),
            dma((sec_count - 1,)),
            dma((sec_count - 1,)),
            dma((sec_count - 1,)),
            dma((sec_count - 1,)),
        ],
        compiler_params=pltpu.CompilerParams(
            collective_id=0, has_side_effects=True, vmem_limit_bytes=40 * 1024 * 1024
        ),
        cost_estimate=pl.CostEstimate(
            flops=2 * 1000 * 1000 * 1000, bytes_accessed=4 * 1024 * 1024, transcendentals=0
        ),
    )(*operands)


def solution(mesh):
    return jax.shard_map(
        per_device,
        mesh=mesh,
        in_specs=(
            P("sec", "tile", None),
            P("sec", "tile", None),
            P("sec", "tile"),
            P("sec", "tile"),
            P("sec", "tile"),
            P("sec", "tile", None),
            P("sec", "tile", None),
            P("sec", "tile"),
            P("sec", "tile"),
            P(),
            P(),
        ),
        out_specs=P("sec", "tile", None),
        check_vma=False,
    )
```

```python
import functools

import jax
import jax.numpy as jnp
from jax import lax
from jax.experimental import pallas as pl
from jax.experimental.pallas import tpu as pltpu
from jax.sharding import PartitionSpec as P

MESH = pl.DeviceIdType.MESH
QUART = 128
GROUP = 4
PAIR = 4
NT = (((1,), (1,)), ((), ()))
F32 = jnp.float32
BF16 = jnp.bfloat16


def offset_value(number, neighbours):
    half = neighbours // 2
    return number - half + 1 if number >= half else number - half


def iota(shape, dim):
    return lax.broadcasted_iota(jnp.int32, shape, dim)


def hot(mask):
    return jnp.where(mask, F32(1.0), F32(0.0)).astype(BF16)


def dot(a, b):
    return jnp.dot(a, b, preferred_element_type=F32)


def dot_nt(a, b):
    return lax.dot_general(a, b, NT, preferred_element_type=F32)


def split_bf16(x):
    high = x.astype(BF16)
    return high, (x - high.astype(F32)).astype(BF16)


def kernel(
    sec_count,
    tile_count,
    neighbours,
    pre_hbm,
    cot_hbm,
    recv_hbm,
    slot_hbm,
    ecnt_smem,
    hmap_hbm,
    dec_hbm,
    dcnt_hbm,
    dnode_hbm,
    wnode_hbm,
    wout_hbm,
    out_ref,
    pre,
    cot,
    recv,
    slot,
    hmaps,
    dec,
    dcnt,
    dnode,
    wnode,
    wout,
    edge_proj,
    slope,
    delta,
    hot_edge,
    hot_sums,
    hot_dec,
    hot_land,
    node_split,
    node_cot,
    base,
    sums,
    dec_out,
    dec_in,
    halo_out,
    halo_in,
    local_out,
    local_in,
    landed_out,
    landed_in,
    load_sem,
    map_send,
    map_recv,
    dec_sem,
    halo_sem,
    local_send,
    local_recv,
    landed_send,
    landed_recv,
):
    edges, latent = cot.shape
    rows = dec.shape[0]
    groups = dec_in.shape[0]
    block = groups // neighbours
    capacity = rows // neighbours
    width = latent // PAIR
    local_rows = sec_count * QUART
    sec = lax.axis_index("sec")
    tile = lax.axis_index("tile")
    others = [lax.rem(sec + k, sec_count) for k in range(sec_count)]
    peers = [
        lax.rem(tile + offset_value(o, neighbours) + tile_count, tile_count)
        for o in range(neighbours)
    ]
    far_first = sorted(range(neighbours), key=lambda o: -abs(offset_value(o, neighbours)))

    far_pairs = sorted(
        ((o, k) for o in range(neighbours) for k in range(sec_count)),
        key=lambda pair: -(
            abs(offset_value(pair[0], neighbours)) / 2 + min(pair[1], sec_count - pair[1])
        ),
    )

    def load(i, src, dst):
        return pltpu.make_async_copy(src, dst, load_sem.at[i])

    first_loads = [load(0, dcnt_hbm, dcnt), load(1, dec_hbm.at[0], dec)]
    edge_loads = [
        load(2, cot_hbm.at[0], cot),
        load(3, wout_hbm, wout),
        load(4, pre_hbm.at[0], pre),
    ]
    index_loads = [
        load(5, recv_hbm, recv),
        load(6, slot_hbm, slot),
        load(7, dnode_hbm, dnode),
        load(8, hmap_hbm.at[0], hmaps.at[sec]),
    ]
    weight_load = load(9, wnode_hbm, wnode)
    for copy in first_loads:
        copy.start()

    barrier = pltpu.get_barrier_semaphore()
    for o in far_first:
        pl.semaphore_signal(barrier, inc=1, device_id=(sec, peers[o]), device_id_type=MESH)
    for other in others[1:]:
        pl.semaphore_signal(barrier, inc=1, device_id=(other, tile), device_id_type=MESH)

    for copy in edge_loads + index_loads + [weight_load]:
        copy.start()

    def over_sec(k, src, dst, send_sem, recv_sem):
        return pltpu.make_async_remote_copy(
            src_ref=src,
            dst_ref=dst,
            send_sem=send_sem.at[k - 1],
            recv_sem=recv_sem.at[k - 1],
            device_id=(others[k], tile),
            device_id_type=MESH,
        )

    def over_tile(o, quarter, src, dst, sem):
        return pltpu.make_async_remote_copy(
            src_ref=src,
            dst_ref=dst,
            send_sem=sem.at[0],
            recv_sem=sem.at[1],
            device_id=(quarter, peers[o]),
            device_id_type=MESH,
        )

    first_loads[0].wait()
    lane = iota((1, rows), 1)
    count = jnp.zeros((1, rows), jnp.int32)
    for o in range(neighbours):
        count = jnp.where(lane // capacity == o, dcnt[0:1, o : o + 1], count)
    live_lane = jnp.where(lane % capacity < count, lane // GROUP, -1)
    pick = hot(iota((groups, rows), 0) == live_lane)
    first_loads[1].wait()
    dec_out[...] = dot(pick, dec[...]).astype(BF16)

    pl.semaphore_wait(barrier, neighbours + sec_count - 1)

    for o in far_first:
        at = pl.ds(o * block, block)
        over_tile(o, sec, dec_out.at[at], dec_in.at[at], dec_sem).start()
    for copy in edge_loads:
        copy.wait()
    step = 256

    def edge_block(i, carry):
        at = pl.ds(i * step, step)
        edge_proj[at, :] = dot_nt(cot[at, :], wout[...])
        v = pre[at, :].astype(F32)
        s = jax.nn.sigmoid(v)
        slope[at, :] = s * (1.0 + v * (1.0 - s))
        return carry

    lax.fori_loop(0, edges // step, edge_block, 0, unroll=True)

    map_copies = [
        over_sec(k, hmap_hbm.at[0], hmaps.at[sec], map_send, map_recv)
        for k in range(1, sec_count)
    ]
    for copy in map_copies:
        copy.start()
    for copy in index_loads:
        copy.wait()
    node_row = iota((QUART, edges), 0)
    receivers = recv[...]
    edge_hot = jnp.where(node_row == receivers, F32(1.0), F32(0.0)).T.astype(BF16)
    hot_edge[:, :QUART] = edge_hot
    hot_edge[:, QUART:] = edge_hot
    live = iota((1, edges), 1) < ecnt_smem[0, 0]
    live_slot = jnp.where(live, slot[...], -1)
    live_recv = jnp.where(live, receivers, -1)
    hot_sums[0:QUART, :] = hot(node_row == live_slot - local_rows)
    for k in range(sec_count):
        hot_sums[(k + 1) * QUART : (k + 2) * QUART, :] = hot(
            node_row == live_slot - others[k] * QUART
        )
    hot_sums[(sec_count + 1) * QUART :, :] = hot(node_row == live_recv)
    first_of_group = jnp.where(lane % GROUP == 0, dnode[...], -1)
    named = hot(iota((QUART, rows), 0) == first_of_group)
    group_of = hot(iota((groups, rows), 0) == lane // GROUP)
    hot_dec[...] = dot_nt(named, group_of).astype(BF16)

    pltpu.make_async_copy(dec_in, dec_in, dec_sem.at[1]).wait()
    cot_sum = dot(hot_dec[...], dec_in[...])
    node_cot[...] = cot_sum
    high, low = split_bf16(dot_nt(cot_sum.astype(BF16), wout[...]))
    node_split[:QUART, :] = high
    node_split[QUART:, :] = low

    def delta_block(i, carry):
        at = pl.ds(i * step, step)
        act = edge_proj[at, :] + dot(hot_edge[at, :], node_split[...])
        delta[at, :] = (act * slope[at, :]).astype(BF16)
        return carry

    lax.fori_loop(0, edges // step, delta_block, 0, unroll=True)

    halo_rows = dot(hot_sums[0:QUART, :], delta[...]).astype(BF16)
    for j in range(PAIR):
        halo_out[j] = halo_rows[:, j * width : (j + 1) * width]
    for o, k in far_pairs:
        at = pl.ds(o * block, block)
        over_tile(
            o, others[k], halo_out.at[others[k], at], halo_in.at[sec, at], halo_sem
        ).start()

    def sum_block(i, carry):
        at = pl.ds(i * QUART, QUART)
        sums[at, :] = dot(hot_sums[pl.ds((i + 1) * QUART, QUART), :], delta[...])
        return carry

    lax.fori_loop(1, sec_count, sum_block, 0, unroll=True)
    local_copies = [
        over_sec(k, local_out.at[k - 1], local_in.at[k - 1], local_send, local_recv)
        for k in range(1, sec_count)
    ]
    for k in range(1, sec_count):
        local_out[k - 1] = sums[k * QUART : (k + 1) * QUART, :].astype(BF16)
        local_copies[k - 1].start()
    sum_block(0, 0)
    sum_block(sec_count, 0)

    for copy in map_copies:
        copy.wait_recv()
    for k in range(sec_count):
        for q in range(PAIR):
            hot_land[k * QUART : (k + 1) * QUART, q * QUART : (q + 1) * QUART] = hot(
                iota((QUART, QUART), 0) == hmaps[q] - others[k] * QUART
            )
    weight_load.wait()
    received = split_bf16(sums[sec_count * QUART :, :])
    base[...] = (
        node_cot[...]
        + dot_nt(received[0], wnode[latent:, :])
        + dot_nt(received[1], wnode[latent:, :])
    )

    pltpu.make_async_copy(halo_in, halo_in, halo_sem.at[1]).wait()
    arrived = halo_in[...].reshape(PAIR * QUART, width)
    landed = dot(hot_land[...], arrived).astype(BF16)
    landed_copies = [
        over_sec(k, landed_out.at[k - 1], landed_in.at[sec], landed_send, landed_recv)
        for k in range(1, sec_count)
    ]
    for k in range(1, sec_count):
        landed_out[k - 1] = landed[k * QUART : (k + 1) * QUART, :]
    for copy in landed_copies:
        copy.start()
    landed_in[sec] = landed[:QUART, :]

    total = sums[:QUART, :]
    for k in range(1, sec_count):
        local_copies[k - 1].wait_recv()
        total += local_in[k - 1].astype(F32)
    sent = split_bf16(total)
    base[...] += dot_nt(sent[0], wnode[:latent, :]) + dot_nt(sent[1], wnode[:latent, :])

    for copy in landed_copies:
        copy.wait_recv()
    columns = jnp.concatenate([landed_in[j] for j in range(sec_count)], axis=1)
    weights = jnp.concatenate([wnode[:latent, :]] * (sec_count // PAIR), axis=1)
    out_ref[0] = base[...] + dot_nt(columns, weights)

    for copy in map_copies + local_copies + landed_copies:
        copy.wait_send()
    pltpu.make_async_copy(dec_out, dec_out, dec_sem.at[0]).wait()
    pltpu.make_async_copy(halo_out, halo_out, halo_sem.at[0]).wait()


def per_device(
    pre_act,
    edge_cot,
    recv_local,
    send_slot,
    edge_count,
    halo_map,
    dec_rows,
    dec_count,
    dec_node,
    w_node,
    w_out,
):
    sec_count = lax.axis_size("sec")
    tile_count = lax.axis_size("tile")
    edges, latent = pre_act.shape[1:]
    rows = dec_rows.shape[1]
    neighbours = dec_count.shape[1]
    groups = rows // GROUP
    halo = halo_map.shape[2]
    width = latent // PAIR
    def hbm(x):
        return pltpu.with_memory_space_constraint(x, pltpu.HBM)

    operands = (
        hbm(pre_act),
        hbm(edge_cot),
        hbm(recv_local),
        hbm(send_slot),
        edge_count,
        hbm(halo_map),
        hbm(dec_rows),
        hbm(dec_count),
        hbm(dec_node),
        hbm(w_node),
        hbm(w_out),
    )
    vmem = pltpu.VMEM
    dma = pltpu.SemaphoreType.DMA
    return pl.pallas_call(
        functools.partial(kernel, sec_count, tile_count, neighbours),
        out_shape=vmem((1, QUART, latent), F32),
        in_specs=[
            pl.BlockSpec(memory_space=pltpu.SMEM if x is edge_count else pl.ANY) for x in operands
        ],
        out_specs=pl.BlockSpec(memory_space=vmem),
        scratch_shapes=[
            vmem((edges, latent), BF16),
            vmem((edges, latent), BF16),
            vmem((1, edges), jnp.int32),
            vmem((1, edges), jnp.int32),
            vmem((PAIR, 1, halo), jnp.int32),
            vmem((rows, latent), BF16),
            vmem((1, neighbours), jnp.int32),
            vmem((1, rows), jnp.int32),
            vmem(w_node.shape, BF16),
            vmem(w_out.shape, BF16),
            vmem((edges, latent), F32),
            vmem((edges, latent), F32),
            vmem((edges, latent), BF16),
            vmem((edges, 2 * QUART), BF16),
            vmem(((sec_count + 2) * QUART, edges), BF16),
            vmem((QUART, groups), BF16),
            vmem((sec_count * QUART, PAIR * halo), BF16),
            vmem((2 * QUART, latent), BF16),
            vmem((QUART, latent), F32),
            vmem((QUART, latent), F32),
            vmem(((sec_count + 1) * QUART, latent), F32),
            vmem((groups, latent), BF16),
            vmem((groups, latent), BF16),
            vmem((PAIR, halo, width), BF16),
            vmem((PAIR, halo, width), BF16),
            vmem((sec_count - 1, QUART, latent), BF16),
            vmem((sec_count - 1, QUART, latent), BF16),
            vmem((sec_count - 1, QUART, width), BF16),
            vmem((sec_count, QUART, width), BF16),
            dma((10,)),
            dma((sec_count - 1,)),
            dma((sec_count - 1,)),
            dma((2,)),
            dma((2,)),
            dma((sec_count - 1,)),
            dma((sec_count - 1,)),
            dma((sec_count - 1,)),
            dma((sec_count - 1,)),
        ],
        compiler_params=pltpu.CompilerParams(
            collective_id=0, has_side_effects=True, vmem_limit_bytes=40 * 1024 * 1024
        ),
        cost_estimate=pl.CostEstimate(
            flops=2 * 1000 * 1000 * 1000, bytes_accessed=4 * 1024 * 1024, transcendentals=0
        ),
    )(*operands)


def solution(mesh):
    return jax.shard_map(
        per_device,
        mesh=mesh,
        in_specs=(
            P("sec", "tile", None),
            P("sec", "tile", None),
            P("sec", "tile"),
            P("sec", "tile"),
            P("sec", "tile"),
            P("sec", "tile", None),
            P("sec", "tile", None),
            P("sec", "tile"),
            P("sec", "tile"),
            P(),
            P(),
        ),
        out_specs=P("sec", "tile", None),
        check_vma=False,
    )
```
